32 devices in a mesh: row: 16 (over z, y, core), col: 2 (over x).
Axes of the slice: x: 2, y: 2, z: 4, core: 2. Of those that a mesh axis runs over, the one named last changes fastest.
Arguments:
- rhs: bfloat16 [262144, 128], P(('row', 'col')), may hold values from -6 to 6
- leaf_basis: bfloat16 [2048, 64, 256], P(('row', 'col')), may hold values from -0.375 to 0.375
- transfer: bfloat16 [4, 16, 2, 64, 64, 256], P(None, 'row', 'col'), may hold values from -0.375 to 0.375
- ranks: int32 [4, 16, 2, 64], P(None, 'row', 'col'), may hold values from 32 to 64, as said below
- out_basis: bfloat16 [16, 64, 128, 128], P('row'), may hold values from -0.375 to 0.375
Outputs:
- result: bfloat16 [131072, 128], P(('row', 'col'))
The draws below stay inside these ranges and needn't reach their ends.
Inputs may be any that keep to these rules, and one draw needn't show every extreme that they name: `ranks`: at every level some block has live rank exactly 64.
All inputs are finite; a program needn't handle non-finite values.
Results may differ from the reference program's by a relative error of at most 0.0014.
Values sent between devices are 32-bit elements; how exact they have to be, the bound alone decides.
A program may use at most 128 MiB of HBM per device.

```python
import jax
import jax.numpy as jnp
from jax import lax

R = 64
K = 64
LEAF = 128
LEVELS = 4
G = 64
LEAVES = 2048
UNKNOWNS = 262144
N_ROW = 16
N_COL = 2


def draw_ranks(key, part):
    key = jax.random.fold_in(key, 7)
    first_key, second_key = jax.random.split(key)
    values = jax.random.randint(first_key, (LEVELS, N_ROW, N_COL, G), K // 2, K + 1)
    chosen = jax.random.randint(second_key, (LEVELS, 1, 1, 1), 0, N_ROW * N_COL * G)
    flat_index = (jnp.arange(N_ROW)[:, None, None] * N_COL + jnp.arange(N_COL)[None, :, None]) * G + jnp.arange(G)[None, None, :]
    return jnp.where(flat_index[None] == chosen, K, values).astype(jnp.int32)


def levels(key, extent, cuts, smallest, largest):
    factor_of, own = 1.0, jax.random.fold_in(key, 6)
    for axis_at, shards_of in cuts:
        heights = jnp.exp(jax.random.uniform(jax.random.fold_in(own, axis_at), (shards_of,), jnp.float32, smallest / len(cuts), largest / len(cuts)))
        factor_of = factor_of * jnp.repeat(heights, extent[axis_at] // shards_of).reshape([-1 if axis == axis_at else 1 for axis in range(len(extent))])
    return factor_of


def bell_draw(own_key, extent, width, reach, cuts=(), kind=jnp.bfloat16):
    values = width * jax.random.normal(own_key, extent, jnp.float32)
    if cuts:
        values = values * levels(own_key, extent, cuts, -0.22, 0.18)
    return jnp.clip(values, -reach, reach).astype(kind)


def setup_inputs(seed: int = 0) -> dict:
    streams_of = jax.random.split(jax.random.key(seed), 6)
    return {
        "rhs": bell_draw(streams_of[0], (UNKNOWNS, 2 * R), 1.0, 6.0, ((0, 32),)),
        "leaf_basis": bell_draw(streams_of[1], (LEAVES, K, 2 * LEAF), (2 * LEAF) ** -0.5, 0.375, ((0, 32),)),
        "transfer": bell_draw(streams_of[2], (LEVELS, N_ROW, N_COL, G, K, 4 * K), (4 * K) ** -0.5, 0.375, ((1, 16), (2, 2))),
        "ranks": draw_ranks(jax.random.fold_in(streams_of[5], 71), 0),
        "out_basis": bell_draw(streams_of[4], (N_ROW, G, LEAF, 2 * K), (2 * K * N_COL) ** -0.5, 0.375, ((0, 16),)),
    }


def complex_stack(block):
    middle = block.shape[-1] // 2
    flipped = jnp.concatenate([-block[..., middle:], block[..., :middle]], -1)
    return jnp.concatenate([block, flipped], -2)


def reference(rhs, leaf_basis, transfer, ranks, out_basis):
    positions = transfer.shape[1]
    columns_count = transfer.shape[2]
    blocks_dev = transfer.shape[3]
    rank_cap = leaf_basis.shape[1]
    points = leaf_basis.shape[2] // 2
    columns = rhs.shape[1]
    half_count = blocks_dev // 2
    sources = rhs.reshape(positions, columns_count * blocks_dev, points, columns)
    bases = leaf_basis.reshape(positions, columns_count * blocks_dev, rank_cap, 2 * points)

    def leaf_apply(pair):
        source, basis = pair
        return jnp.einsum('gkm,gmn->gkn', basis.astype(jnp.float32), complex_stack(source.astype(jnp.float32)), precision=lax.Precision.HIGHEST)

    coeff = lax.map(leaf_apply, (sources, bases))
    coeff = coeff.reshape(positions, columns_count, blocks_dev, rank_cap, columns)
    index = jnp.arange(positions, dtype=jnp.int32)
    for level in range(transfer.shape[0]):
        upper_bit = ((index >> level) & 1)[:, None, None, None, None]
        partner = index ^ (1 << level)
        halves = coeff.reshape(positions, columns_count, 2, half_count, rank_cap, columns)
        kept_half = jnp.where(upper_bit == 1, halves[:, :, 1], halves[:, :, 0])
        other = halves[partner]
        partner_half = jnp.where(upper_bit == 1, other[:, :, 1], other[:, :, 0])
        stacked = jnp.concatenate([complex_stack(kept_half), complex_stack(partner_half)], -2)
        matrices = transfer[level].astype(jnp.float32).reshape(positions, columns_count, half_count, 2, rank_cap, 4 * rank_cap)
        mixed = jnp.einsum('pcjskm,pcjmn->pcjskn', matrices, stacked, precision=lax.Precision.HIGHEST)
        mixed = mixed.reshape(positions, columns_count, blocks_dev, rank_cap, columns)
        live_rows = jnp.arange(rank_cap, dtype=jnp.int32)[None, None, None, :] < ranks[level][..., None]
        coeff = jnp.where(live_rows[..., None], mixed, jnp.float32(0.0))
    total = jnp.sum(coeff, axis=1)
    result = jnp.einsum('pglm,pgmn->pgln', out_basis.astype(jnp.float32), complex_stack(total), precision=lax.Precision.HIGHEST)
    return result.reshape(positions * blocks_dev * points, columns).astype(jnp.bfloat16)
```

```python
import functools

import jax
import jax.numpy as jnp
from jax import lax
from jax.experimental import pallas as pl
from jax.experimental.pallas import tpu as pltpu
from jax.sharding import PartitionSpec as P

MESH = pl.DeviceIdType.MESH
F32 = jnp.float32
BF16 = jnp.bfloat16


def rotated(z):
    middle = z.shape[1] // 2
    lane = lax.broadcasted_iota(jnp.int32, z.shape, 1)
    turned = pltpu.roll(z, middle, 1)
    return jnp.where(lane < middle, -turned, turned)


def split_dot(matrix, stacked):
    high = stacked.astype(BF16)
    low = (stacked - high.astype(F32)).astype(BF16)
    both = jnp.dot(matrix, jnp.concatenate([high, low], 1), preferred_element_type=F32)
    columns = stacked.shape[1]
    return both[:, :columns] + both[:, columns:]


def kernel(
    sizes, ranks, rhs_hbm, leaf_hbm, transfer_hbm, basis_hbm, result_hbm,
    rhs, leaf, transfer, basis, result, coeff, arrived, shared,
    load_sem, out_sem, send_sem, recv_sem, share_send, share_recv,
):
    levels, chunks, owned, n_col, points, rank_cap = sizes
    block_count = 1 << levels
    half = block_count // 2
    quarter = half // 2
    p = lax.axis_index("row")
    c = lax.axis_index("col")
    bits = [(p // (1 << level)) % 2 for level in range(levels)] + [1]
    partners = [p + (1 - 2 * bits[level]) * (1 << level) for level in range(levels)]
    piece = min(block_count, owned)
    own_chunks = max(1, chunks // n_col)
    first = (c * chunks) // n_col + own_chunks
    order = [(first + n) % chunks for n in range(chunks)]

    loads = {}

    def load(name, source, target):
        copy = pltpu.make_async_copy(source, target, load_sem.at[len(loads)])
        copy.start()
        loads[name] = copy

    for n in range(chunks):
        load(("rhs", n), rhs_hbm.at[:, order[n]], rhs.at[n])
        load(("leaf", n), leaf_hbm.at[:, order[n]], leaf.at[n])
        if n == 0:
            load(("transfer", 0), transfer_hbm.at[0], transfer.at[0])
    for level in range(1, levels):
        load(("transfer", level), transfer_hbm.at[level], transfer.at[level])
    load("basis", basis_hbm.at[pl.ds(c * owned, owned)], basis)

    barrier = pltpu.get_barrier_semaphore()
    for level in range(levels):
        pl.semaphore_signal(barrier, 1, device_id={"row": partners[level]}, device_id_type=MESH)
    for step in range(1, n_col):
        pl.semaphore_signal(barrier, 1, device_id={"col": (c + step) % n_col}, device_id_type=MESH)
    pl.semaphore_wait(barrier, levels + n_col - 1)

    waited = set()

    def loaded(name):
        if name not in waited:
            waited.add(name)
            loads[name].wait()

    def part(level, h):
        if level == levels - 1:
            return h
        return 1 - bits[level + 1] if h == 0 else bits[level + 1]

    def exchange(level, n, h):
        at = part(level, h) * quarter
        return pltpu.make_async_remote_copy(
            src_ref=coeff.at[level, n, pl.ds((1 - bits[level]) * half + at, quarter)],
            dst_ref=arrived.at[level, n, pl.ds(at, quarter)],
            send_sem=send_sem.at[level, n, h],
            recv_sem=recv_sem.at[level, n, h],
            device_id={"row": partners[level]},
            device_id_type=MESH,
        )

    def leaf_block(n, f):
        z = rhs[n, f].astype(F32)
        stacked = jnp.concatenate([z, rotated(z)], 0).astype(BF16)
        coeff[0, n, f] = jnp.dot(leaf[n, f], stacked, preferred_element_type=F32)

    def leaf_blocks(n, start, count):
        def body(i, carry):
            leaf_block(n, start + 2 * i)
            leaf_block(n, start + 2 * i + 1)
            return carry

        lax.fori_loop(0, count // 2, body, 0)

    def mix_block(level, n, m):
        low = m % (1 << level)
        high = m // (1 << level)
        j = high * (chunks << level) + order[n] * (1 << level) + low
        own = coeff[level, n, bits[level] * half + m]
        other = arrived[level, n, m]
        stacked = jnp.concatenate([own, rotated(own), other, rotated(other)], 0)
        mixed = split_dot(transfer[level, j], stacked)
        row = lax.broadcasted_iota(jnp.int32, (rank_cap, mixed.shape[1]), 0)
        for s in range(2):
            live = row < ranks[level, 2 * j + s]
            coeff[level + 1, n, 2 * m + s] = jnp.where(
                live, mixed[s * rank_cap : (s + 1) * rank_cap], 0.0
            )

    def mix_blocks(level, n, start, count):
        def body(i, carry):
            mix_block(level, n, start + 2 * i)
            mix_block(level, n, start + 2 * i + 1)
            return carry

        if count == 2:
            body(0, 0)
        else:
            lax.fori_loop(0, count // 2, body, 0)

    def leaves_of(n):
        loaded(("rhs", n))
        loaded(("leaf", n))
        sent = (1 - bits[0]) * half
        for h in range(2):
            leaf_blocks(n, sent + part(0, h) * quarter, quarter)
            exchange(0, n, h).start()
        leaf_blocks(n, bits[0] * half, half)

    def mix(level, n):
        loaded(("transfer", level))
        for h in range(2):
            exchange(level, n, h).wait_recv()
            start = part(level, h) * quarter
            if h == 0 and level + 1 < levels:
                for k in range(2):
                    mix_blocks(level, n, start + part(level + 1, k) * (quarter // 2), quarter // 2)
                    exchange(level + 1, n, k).start()
            else:
                mix_blocks(level, n, start, quarter)

    def share(n, k):
        g = order[n] * block_count + k * piece
        owner = g // owned
        slot = (g % owned) // piece
        return owner, pltpu.make_async_remote_copy(
            src_ref=coeff.at[levels, n, pl.ds(k * piece, piece)],
            dst_ref=shared.at[c, pl.ds(slot * piece, piece)],
            send_sem=share_send.at[n, k],
            recv_sem=share_recv.at[c, slot],
            device_id={"col": owner},
            device_id_type=MESH,
        )

    pieces = block_count // piece

    def each_share(act):
        for n in range(chunks):
            act_on_share(n, act)

    def act_on_share(n, act):
        if chunks >= n_col:
            if n < chunks - own_chunks:
                act(share(n, 0)[1])
            return
        for k in range(pieces):
            owner, copy = share(n, k)

            @pl.when(owner != c)
            def _():
                act(copy)

    def share_out(n):
        act_on_share(n, lambda copy: copy.start())

    def receive_shares(slot):
        for step in range(1, n_col):
            sender = (c + step) % n_col
            pltpu.make_async_remote_copy(
                src_ref=coeff.at[levels, 0, pl.ds(0, piece)],
                dst_ref=shared.at[sender, pl.ds(slot * piece, piece)],
                send_sem=share_send.at[0, 0],
                recv_sem=share_recv.at[sender, slot],
                device_id={"col": sender},
                device_id_type=MESH,
            ).wait_recv()

    def target_block(n, f, g):
        total = coeff[levels, n, f]
        for step in range(1, n_col):
            total = total + shared[(c + step) % n_col, g]
        stacked = jnp.concatenate([total, rotated(total)], 0)
        result[g] = split_dot(basis[g], stacked).astype(BF16)

    def targets_of(n):
        loaded("basis")
        slot = n - (chunks - own_chunks)
        receive_shares(slot)
        begin = 0
        if chunks < n_col:
            begin = (c * owned) % block_count

        def body(i, carry):
            for u in range(2):
                f = 2 * i + u
                target_block(n, begin + f, slot * piece + f)
            return carry

        lax.fori_loop(0, piece // 2, body, 0)
        copy = pltpu.make_async_copy(
            result.at[pl.ds(slot * piece, piece)],
            result_hbm.at[pl.ds(slot * piece, piece)],
            out_sem.at[slot],
        )
        copy.start()
        return copy

    finals = []

    def run(stage, n):
        if stage == 0:
            leaves_of(n)
            return
        mix(stage - 1, n)
        if stage == levels:
            share_out(n)
            if n >= chunks - own_chunks:
                finals.append(targets_of(n))

    plan = []
    placed = set()

    def place(stage, n):
        if 0 <= n < chunks and 0 <= stage <= levels and (stage, n) not in placed:
            placed.add((stage, n))
            plan.append((stage, n))

    for stage, n in (
        (0, 0), (0, 1), (1, 0), (0, 2), (1, 1), (2, 0), (1, 2), (0, 3), (3, 0),
        (1, 3), (2, 1), (3, 1), (2, 2), (2, 3), (3, 2), (3, 3),
    ):
        place(stage, n)
    for stage in range(levels + 1):
        for n in range(chunks):
            place(stage, n)
    for stage, n in plan:
        run(stage, n)

    for level in range(levels):
        for n in range(chunks):
            for h in range(2):
                exchange(level, n, h).wait_send()
    each_share(lambda copy: copy.wait_send())
    for copy in finals:
        copy.wait()


def shards(rhs, leaf_basis, transfer, ranks, out_basis):
    leaves, rank_cap, width = leaf_basis.shape
    points = width // 2
    columns = rhs.shape[1]
    levels = transfer.shape[0]
    n_col = lax.axis_size("col")
    owned = leaves // n_col
    block_count = 1 << levels
    half = block_count // 2
    chunks = leaves // block_count
    piece = min(block_count, owned)
    sizes = (levels, chunks, owned, n_col, points, rank_cap)
    any_space = pl.BlockSpec(memory_space=pl.ANY)
    result = pl.pallas_call(
        functools.partial(kernel, sizes),
        out_shape=jax.ShapeDtypeStruct((owned, points, columns), BF16),
        in_specs=[pl.BlockSpec(memory_space=pltpu.SMEM)] + [any_space] * 4,
        out_specs=any_space,
        scratch_shapes=[
            pltpu.VMEM((chunks, block_count, points, columns), BF16),
            pltpu.VMEM((chunks, block_count, rank_cap, width), BF16),
            pltpu.VMEM((levels, leaves // 2, 2 * rank_cap, 4 * rank_cap), BF16),
            pltpu.VMEM((owned, points, 2 * rank_cap), BF16),
            pltpu.VMEM((owned, points, columns), BF16),
            pltpu.VMEM((levels + 1, chunks, block_count, rank_cap, columns), F32),
            pltpu.VMEM((levels, chunks, half, rank_cap, columns), F32),
            pltpu.VMEM((n_col, owned, rank_cap, columns), F32),
            pltpu.SemaphoreType.DMA((2 * chunks + levels + 1,)),
            pltpu.SemaphoreType.DMA((owned // piece,)),
            pltpu.SemaphoreType.DMA((levels, chunks, 2)),
            pltpu.SemaphoreType.DMA((levels, chunks, 2)),
            pltpu.SemaphoreType.DMA((chunks, block_count // piece)),
            pltpu.SemaphoreType.DMA((n_col, owned // piece)),
        ],
        compiler_params=pltpu.CompilerParams(
            collective_id=0, has_side_effects=True, vmem_limit_bytes=48 * 1024 * 1024
        ),
    )(
        ranks.reshape(levels, leaves),
        rhs.reshape(block_count, chunks, points, columns),
        leaf_basis.reshape(block_count, chunks, rank_cap, width),
        transfer.reshape(levels, leaves // 2, 2 * rank_cap, 4 * rank_cap),
        out_basis.reshape(leaves, points, 2 * rank_cap),
    )
    return result.reshape(owned * points, columns)


def solution(mesh):
    in_specs = (
        P(("row", "col"), None),
        P(("row", "col"), None, None),
        P(None, "row", "col", None, None, None),
        P(None, "row", "col", None),
        P("row", None, None, None),
    )
    out_specs = P(("row", "col"), None)
    return jax.shard_map(shards, mesh=mesh, in_specs=in_specs, out_specs=out_specs, check_vma=False)
```

```python
import functools

import jax
import jax.numpy as jnp
from jax import lax
from jax.experimental import pallas as pl
from jax.experimental.pallas import tpu as pltpu
from jax.sharding import PartitionSpec as P

MESH = pl.DeviceIdType.MESH
F32 = jnp.float32
BF16 = jnp.bfloat16
PLAN = (
    (0, 0, 0), (0, 0, 1), (0, 1, 0), (1, 0, 0), (1, 0, 1), (0, 1, 1),
    (1, 1, 0), (1, 1, 1), (2, 0, 0), (0, 2, 0), (0, 2, 1), (2, 0, 1),
    (1, 2, 0), (3, 0, 0), (2, 1, 0), (1, 2, 1), (3, 0, 1), (2, 1, 1),
    (0, 3, 0), (2, 2, 0), (0, 3, 1), (1, 3, 0), (2, 2, 1), (1, 3, 1),
    (4, 0, 0), (2, 3, 0), (3, 1, 0), (4, 0, 1), (2, 3, 1), (3, 1, 1),
    (3, 2, 0), (4, 1, 0), (3, 2, 1), (3, 3, 0), (4, 1, 1), (3, 3, 1),
    (4, 2, 0), (4, 2, 1), (5, 2, 0), (4, 3, 0), (4, 3, 1), (5, 3, 0),
)


def rotated(z):
    middle = z.shape[1] // 2
    lane = lax.broadcasted_iota(jnp.int32, z.shape, 1)
    turned = pltpu.roll(z, middle, 1)
    return jnp.where(lane < middle, -turned, turned)


def split_dot(matrix, stacked):
    high = stacked.astype(BF16)
    low = (stacked - high.astype(F32)).astype(BF16)
    both = jnp.dot(matrix, jnp.concatenate([high, low], 1), preferred_element_type=F32)
    columns = stacked.shape[1]
    return both[:, :columns] + both[:, columns:]


def kernel(
    sizes, ranks, rhs_hbm, leaf_hbm, transfer_hbm, basis_hbm, result_hbm,
    rhs, leaf, transfer, basis, result, coeff, arrived, shared,
    load_sem, out_sem, send_sem, recv_sem, share_send, share_recv,
):
    levels, chunks, owned, n_col, points, rank_cap = sizes
    block_count = 1 << levels
    half = block_count // 2
    quarter = half // 2
    p = lax.axis_index("row")
    c = lax.axis_index("col")
    bits = [(p // (1 << level)) % 2 for level in range(levels)] + [1]
    partners = [p + (1 - 2 * bits[level]) * (1 << level) for level in range(levels)]
    piece = min(block_count, owned)
    own_chunks = max(1, chunks // n_col)
    first = (c * chunks) // n_col + own_chunks
    order = [(first + n) % chunks for n in range(chunks)]

    loads = {}

    def load(name, source, target):
        copy = pltpu.make_async_copy(source, target, load_sem.at[len(loads)])
        copy.start()
        loads[name] = copy

    for n in range(chunks):
        load(("rhs", n), rhs_hbm.at[:, order[n]], rhs.at[n])
        load(("leaf", n), leaf_hbm.at[:, order[n]], leaf.at[n])
        if n == 0:
            load(("transfer", 0), transfer_hbm.at[0], transfer.at[0])
    for level in range(1, levels):
        load(("transfer", level), transfer_hbm.at[level], transfer.at[level])
    load("basis", basis_hbm.at[pl.ds(c * owned, owned)], basis)

    barrier = pltpu.get_barrier_semaphore()
    for level in range(levels):
        pl.semaphore_signal(barrier, 1, device_id={"row": partners[level]}, device_id_type=MESH)
    for step in range(1, n_col):
        pl.semaphore_signal(barrier, 1, device_id={"col": (c + step) % n_col}, device_id_type=MESH)
    pl.semaphore_wait(barrier, levels + n_col - 1)

    waited = set()

    def loaded(name):
        if name not in waited:
            waited.add(name)
            loads[name].wait()

    def part(level, h):
        if level == levels - 1:
            return h
        return 1 - bits[level + 1] if h == 0 else bits[level + 1]

    def exchange(level, n, h):
        at = part(level, h) * quarter
        return pltpu.make_async_remote_copy(
            src_ref=coeff.at[level, n, pl.ds((1 - bits[level]) * half + at, quarter)],
            dst_ref=arrived.at[level, n, pl.ds(at, quarter)],
            send_sem=send_sem.at[level, n, h],
            recv_sem=recv_sem.at[level, n, h],
            device_id={"row": partners[level]},
            device_id_type=MESH,
        )

    def in_loop(count, act):
        width = min(4, count)

        def body(i, carry):
            stores = [act(width * i + u) for u in range(width)]
            for ref, rows in stores:
                for at, block in rows:
                    ref[at] = block
            return carry

        if count == width:
            body(0, 0)
        else:
            lax.fori_loop(0, count // width, body, 0)

    def leaf_block(n, f):
        matrix = leaf[n, f]
        parts = jnp.concatenate([matrix[:, :points], matrix[:, points:]], 0)
        both = jnp.dot(parts, rhs[n, f], preferred_element_type=F32)
        return coeff, [((0, n, f), both[:rank_cap] + rotated(both[rank_cap:]))]

    def leaf_blocks(n, start, count):
        in_loop(count, lambda i: leaf_block(n, start + i))

    def mix_block(level, n, m):
        low = m % (1 << level)
        high = m // (1 << level)
        j = high * (chunks << level) + order[n] * (1 << level) + low
        own = coeff[level, n, bits[level] * half + m]
        other = arrived[level, n, m]
        stacked = jnp.concatenate([own, rotated(own), other, rotated(other)], 0)
        mixed = split_dot(transfer[level, j], stacked)
        row = lax.broadcasted_iota(jnp.int32, (rank_cap, mixed.shape[1]), 0)
        rows = []
        for s in range(2):
            live = row < ranks[level, 2 * j + s]
            block = jnp.where(live, mixed[s * rank_cap : (s + 1) * rank_cap], 0.0)
            rows.append(((level + 1, n, 2 * m + s), block))
        return coeff, rows

    def mix_blocks(level, n, start, count):
        in_loop(count, lambda i: mix_block(level, n, start + i))

    def leaves_of(n, h):
        loaded(("rhs", n))
        loaded(("leaf", n))
        if h == 1:
            leaf_blocks(n, bits[0] * half, half)
            return
        sent = (1 - bits[0]) * half
        for k in range(2):
            leaf_blocks(n, sent + part(0, k) * quarter, quarter)
            exchange(0, n, k).start()

    def mix(level, n, h):
        loaded(("transfer", level))
        exchange(level, n, h).wait_recv()
        start = part(level, h) * quarter
        if h == 1 or level + 1 == levels:
            mix_blocks(level, n, start, quarter)
            return
        for k in range(2):
            mix_blocks(level, n, start + part(level + 1, k) * (quarter // 2), quarter // 2)
            exchange(level + 1, n, k).start()

    def share(n, k):
        g = order[n] * block_count + k * piece
        owner = g // owned
        slot = (g % owned) // piece
        return owner, pltpu.make_async_remote_copy(
            src_ref=coeff.at[levels, n, pl.ds(k * piece, piece)],
            dst_ref=shared.at[c, pl.ds(slot * piece, piece)],
            send_sem=share_send.at[n, k],
            recv_sem=share_recv.at[c, slot],
            device_id={"col": owner},
            device_id_type=MESH,
        )

    pieces = block_count // piece

    def each_share(act):
        for n in range(chunks):
            act_on_share(n, act)

    def act_on_share(n, act):
        if chunks >= n_col:
            if n < chunks - own_chunks:
                act(share(n, 0)[1])
            return
        for k in range(pieces):
            owner, copy = share(n, k)

            @pl.when(owner != c)
            def _():
                act(copy)

    def share_out(n):
        act_on_share(n, lambda copy: copy.start())

    def receive_shares(slot):
        for step in range(1, n_col):
            sender = (c + step) % n_col
            pltpu.make_async_remote_copy(
                src_ref=coeff.at[levels, 0, pl.ds(0, piece)],
                dst_ref=shared.at[sender, pl.ds(slot * piece, piece)],
                send_sem=share_send.at[0, 0],
                recv_sem=share_recv.at[sender, slot],
                device_id={"col": sender},
                device_id_type=MESH,
            ).wait_recv()

    def target_block(n, f, g):
        total = coeff[levels, n, f]
        for step in range(1, n_col):
            total = total + shared[(c + step) % n_col, g]
        stacked = jnp.concatenate([total, rotated(total)], 0)
        return result, [(g, split_dot(basis[g], stacked).astype(BF16))]

    def targets_of(n):
        loaded("basis")
        slot = n - (chunks - own_chunks)
        receive_shares(slot)
        begin = 0
        if chunks < n_col:
            begin = (c * owned) % block_count

        in_loop(piece, lambda i: target_block(n, begin + i, slot * piece + i))
        copy = pltpu.make_async_copy(
            result.at[pl.ds(slot * piece, piece)],
            result_hbm.at[pl.ds(slot * piece, piece)],
            out_sem.at[slot],
        )
        copy.start()
        return copy

    finals = []

    def run(stage, n, h):
        if stage == 0:
            leaves_of(n, h)
        elif stage <= levels:
            mix(stage - 1, n, h)
            if stage == levels and h == 1:
                share_out(n)
        elif n >= chunks - own_chunks:
            finals.append(targets_of(n))

    plan = list(PLAN) if (levels, chunks) == (4, 4) else []
    for stage in range(levels + 2):
        for n in range(chunks):
            for h in range(1 if stage > levels else 2):
                if (stage, n, h) not in plan:
                    plan.append((stage, n, h))
    for stage, n, h in plan:
        run(stage, n, h)

    for level in range(levels):
        for n in range(chunks):
            for h in range(2):
                exchange(level, n, h).wait_send()
    each_share(lambda copy: copy.wait_send())
    for copy in finals:
        copy.wait()


def shards(rhs, leaf_basis, transfer, ranks, out_basis):
    leaves, rank_cap, width = leaf_basis.shape
    points = width // 2
    columns = rhs.shape[1]
    levels = transfer.shape[0]
    n_col = lax.axis_size("col")
    owned = leaves // n_col
    block_count = 1 << levels
    half = block_count // 2
    chunks = leaves // block_count
    piece = min(block_count, owned)
    sizes = (levels, chunks, owned, n_col, points, rank_cap)
    any_space = pl.BlockSpec(memory_space=pl.ANY)
    result = pl.pallas_call(
        functools.partial(kernel, sizes),
        out_shape=jax.ShapeDtypeStruct((owned, points, columns), BF16),
        in_specs=[pl.BlockSpec(memory_space=pltpu.SMEM)] + [any_space] * 4,
        out_specs=any_space,
        scratch_shapes=[
            pltpu.VMEM((chunks, block_count, points, columns), BF16),
            pltpu.VMEM((chunks, block_count, rank_cap, width), BF16),
            pltpu.VMEM((levels, leaves // 2, 2 * rank_cap, 4 * rank_cap), BF16),
            pltpu.VMEM((owned, points, 2 * rank_cap), BF16),
            pltpu.VMEM((owned, points, columns), BF16),
            pltpu.VMEM((levels + 1, chunks, block_count, rank_cap, columns), F32),
            pltpu.VMEM((levels, chunks, half, rank_cap, columns), F32),
            pltpu.VMEM((n_col, owned, rank_cap, columns), F32),
            pltpu.SemaphoreType.DMA((2 * chunks + levels + 1,)),
            pltpu.SemaphoreType.DMA((owned // piece,)),
            pltpu.SemaphoreType.DMA((levels, chunks, 2)),
            pltpu.SemaphoreType.DMA((levels, chunks, 2)),
            pltpu.SemaphoreType.DMA((chunks, block_count // piece)),
            pltpu.SemaphoreType.DMA((n_col, owned // piece)),
        ],
        compiler_params=pltpu.CompilerParams(
            collective_id=0, has_side_effects=True, vmem_limit_bytes=56 * 1024 * 1024
        ),
    )(
        ranks.reshape(levels, leaves),
        rhs.reshape(block_count, chunks, points, columns),
        leaf_basis.reshape(block_count, chunks, rank_cap, width),
        transfer.reshape(levels, leaves // 2, 2 * rank_cap, 4 * rank_cap),
        out_basis.reshape(leaves, points, 2 * rank_cap),
    )
    return result.reshape(owned * points, columns)


def solution(mesh):
    in_specs = (
        P(("row", "col"), None),
        P(("row", "col"), None, None),
        P(None, "row", "col", None, None, None),
        P(None, "row", "col", None),
        P("row", None, None, None),
    )
    out_specs = P(("row", "col"), None)
    return jax.shard_map(shards, mesh=mesh, in_specs=in_specs, out_specs=out_specs, check_vma=False)
```

```python
import functools

import jax
import jax.numpy as jnp
from jax import lax
from jax.experimental import pallas as pl
from jax.experimental.pallas import tpu as pltpu
from jax.sharding import PartitionSpec as P

MESH = pl.DeviceIdType.MESH
F32 = jnp.float32
BF16 = jnp.bfloat16
PLAN = (
    (0, 0, 0), (0, 0, 1), (0, 1, 0), (1, 0, 0), (1, 0, 1), (0, 1, 1),
    (1, 1, 0), (1, 1, 1), (0, 2, 0), (2, 0, 0), (0, 2, 1), (1, 2, 0),
    (2, 0, 1), (1, 2, 1), (0, 3, 0), (3, 0, 0), (2, 1, 0), (0, 3, 1),
    (1, 3, 0), (1, 3, 1), (2, 1, 1), (2, 2, 0), (2, 2, 1), (2, 3, 0),
    (3, 0, 1), (4, 0, 0), (4, 0, 1), (2, 3, 1), (3, 1, 0), (3, 2, 0),
    (3, 3, 0), (3, 1, 1), (4, 1, 0), (4, 1, 1), (3, 2, 1), (4, 2, 0),
    (4, 2, 1), (5, 2, 0), (5, 2, 1), (3, 3, 1), (4, 3, 0), (4, 3, 1),
    (5, 3, 0), (5, 3, 1),
)


def rotated(z):
    middle = z.shape[1] // 2
    lane = lax.broadcasted_iota(jnp.int32, z.shape, 1)
    turned = pltpu.roll(z, middle, 1)
    return jnp.where(lane < middle, -turned, turned)


def split_dot(matrix, stacked):
    high = stacked.astype(BF16)
    low = (stacked - high.astype(F32)).astype(BF16)
    both = jnp.dot(matrix, jnp.concatenate([high, low], 1), preferred_element_type=F32)
    columns = stacked.shape[1]
    return both[:, :columns] + both[:, columns:]


def kernel(
    sizes, ranks, rhs_hbm, leaf_hbm, transfer_hbm, basis_hbm, result_hbm,
    rhs, leaf, transfer, basis, result, coeff, arrived, shared,
    load_sem, out_sem, send_sem, recv_sem, share_send, share_recv,
):
    levels, chunks, owned, n_col, points, rank_cap = sizes
    block_count = 1 << levels
    half = block_count // 2
    quarter = half // 2
    p = lax.axis_index("row")
    c = lax.axis_index("col")
    bits = [(p // (1 << level)) % 2 for level in range(levels)] + [1]
    partners = [p + (1 - 2 * bits[level]) * (1 << level) for level in range(levels)]
    piece = min(block_count, owned)
    own_chunks = max(1, chunks // n_col)
    first = (c * chunks) // n_col + own_chunks
    order = [(first + n) % chunks for n in range(chunks)]

    loads = {}

    def load(name, source, target):
        copy = pltpu.make_async_copy(source, target, load_sem.at[len(loads)])
        copy.start()
        loads[name] = copy

    for n in range(chunks):
        load(("rhs", n), rhs_hbm.at[:, order[n]], rhs.at[n])
        load(("leaf", n), leaf_hbm.at[:, order[n]], leaf.at[n])
        if n == 0:
            load(("transfer", 0), transfer_hbm.at[0], transfer.at[0])
    for level in range(1, levels):
        load(("transfer", level), transfer_hbm.at[level], transfer.at[level])
    load("basis", basis_hbm.at[pl.ds(c * owned, owned)], basis)

    barrier = pltpu.get_barrier_semaphore()
    for level in range(levels):
        pl.semaphore_signal(barrier, 1, device_id={"row": partners[level]}, device_id_type=MESH)
    for step in range(1, n_col):
        pl.semaphore_signal(barrier, 1, device_id={"col": (c + step) % n_col}, device_id_type=MESH)
    pl.semaphore_wait(barrier, levels + n_col - 1)

    waited = set()

    def loaded(name):
        if name not in waited:
            waited.add(name)
            loads[name].wait()

    def part(level, h):
        if level == levels - 1:
            return h
        return 1 - bits[level + 1] if h == 0 else bits[level + 1]

    def exchange(level, n, h):
        count = 2 if n == 0 and 0 < level < levels - 1 else 1
        size = quarter // count
        copies = []
        for k in range(count):
            at = part(level, h) * quarter + (part(level + 1, k) * size if count == 2 else 0)
            copies.append(
                pltpu.make_async_remote_copy(
                    src_ref=coeff.at[level, n, pl.ds((1 - bits[level]) * half + at, size)],
                    dst_ref=arrived.at[level, n, pl.ds(at, size)],
                    send_sem=send_sem.at[level, n, h, k],
                    recv_sem=recv_sem.at[level, n, h, k],
                    device_id={"row": partners[level]},
                    device_id_type=MESH,
                )
            )
        return copies

    def send(level, n, h):
        for copy in exchange(level, n, h):
            copy.start()

    def in_loop(count, act):
        width = min(4, count)

        def body(i, carry):
            stores = [act(width * i + u) for u in range(width)]
            for ref, rows in stores:
                for at, block in rows:
                    ref[at] = block
            return carry

        if count == width:
            body(0, 0)
        else:
            lax.fori_loop(0, count // width, body, 0)

    def leaf_block(n, f):
        matrix = leaf[n, f]
        parts = jnp.concatenate([matrix[:, :points], matrix[:, points:]], 0)
        both = jnp.dot(parts, rhs[n, f], preferred_element_type=F32)
        return coeff, [((0, n, f), both[:rank_cap] + rotated(both[rank_cap:]))]

    def leaf_blocks(n, start, count):
        in_loop(count, lambda i: leaf_block(n, start + i))

    def mix_block(level, n, m):
        low = m % (1 << level)
        high = m // (1 << level)
        j = high * (chunks << level) + order[n] * (1 << level) + low
        own = coeff[level, n, bits[level] * half + m]
        other = arrived[level, n, m]
        stacked = jnp.concatenate([own, rotated(own), other, rotated(other)], 0)
        mixed = split_dot(transfer[level, j], stacked)
        row = lax.broadcasted_iota(jnp.int32, (rank_cap, mixed.shape[1]), 0)
        rows = []
        for s in range(2):
            live = row < ranks[level, 2 * j + s]
            block = jnp.where(live, mixed[s * rank_cap : (s + 1) * rank_cap], 0.0)
            rows.append(((level + 1, n, 2 * m + s), block))
        return coeff, rows

    def mix_blocks(level, n, start, count):
        in_loop(count, lambda i: mix_block(level, n, start + i))

    def leaves_of(n, h):
        loaded(("rhs", n))
        loaded(("leaf", n))
        if h == 1:
            leaf_blocks(n, bits[0] * half, half)
            return
        sent = (1 - bits[0]) * half
        for k in range(2):
            leaf_blocks(n, sent + part(0, k) * quarter, quarter)
            send(0, n, k)

    def mix(level, n, h):
        loaded(("transfer", level))
        copies = exchange(level, n, h)
        start = part(level, h) * quarter
        if h == 1 or level + 1 == levels:
            for copy in copies:
                copy.wait_recv()
            mix_blocks(level, n, start, quarter)
            return
        for k in range(2):
            if k < len(copies):
                copies[k].wait_recv()
            mix_blocks(level, n, start + part(level + 1, k) * (quarter // 2), quarter // 2)
            if k == 0 or level + 1 != levels - 2:
                send(level + 1, n, k)
        if level == levels - 2:
            send(level, n, 1)

    def share(n, k):
        g = order[n] * block_count + k * piece
        owner = g // owned
        slot = (g % owned) // piece
        return owner, pltpu.make_async_remote_copy(
            src_ref=coeff.at[levels, n, pl.ds(k * piece, piece)],
            dst_ref=shared.at[c, pl.ds(slot * piece, piece)],
            send_sem=share_send.at[n, k],
            recv_sem=share_recv.at[c, slot],
            device_id={"col": owner},
            device_id_type=MESH,
        )

    pieces = block_count // piece

    def each_share(act):
        for n in range(chunks):
            act_on_share(n, act)

    def act_on_share(n, act):
        if chunks >= n_col:
            if n < chunks - own_chunks:
                act(share(n, 0)[1])
            return
        for k in range(pieces):
            owner, copy = share(n, k)

            @pl.when(owner != c)
            def _():
                act(copy)

    def share_out(n):
        act_on_share(n, lambda copy: copy.start())

    def receive_shares(slot):
        for step in range(1, n_col):
            sender = (c + step) % n_col
            pltpu.make_async_remote_copy(
                src_ref=coeff.at[levels, 0, pl.ds(0, piece)],
                dst_ref=shared.at[sender, pl.ds(slot * piece, piece)],
                send_sem=share_send.at[0, 0],
                recv_sem=share_recv.at[sender, slot],
                device_id={"col": sender},
                device_id_type=MESH,
            ).wait_recv()

    def target_block(n, f, g):
        total = coeff[levels, n, f]
        for step in range(1, n_col):
            total = total + shared[(c + step) % n_col, g]
        stacked = jnp.concatenate([total, rotated(total)], 0)
        return result, [(g, split_dot(basis[g], stacked).astype(BF16))]

    def targets_of(n, h):
        slot = n - (chunks - own_chunks)
        begin, count = h * half, half
        if piece < block_count:
            if h == 0:
                return
            begin, count = (c * owned) % block_count, piece
        if h == 0 or piece < block_count:
            loaded("basis")
            receive_shares(slot)
        g = slot * piece + (h * half if piece == block_count else 0)
        in_loop(count, lambda i: target_block(n, begin + i, g + i))
        copy = pltpu.make_async_copy(
            result.at[pl.ds(g, count)], result_hbm.at[pl.ds(g, count)], out_sem.at[slot, h]
        )
        copy.start()
        finals.append(copy)

    finals = []

    def run(stage, n, h):
        if stage == 0:
            leaves_of(n, h)
        elif stage <= levels:
            mix(stage - 1, n, h)
            if stage == levels and h == 1:
                share_out(n)
        elif n >= chunks - own_chunks:
            targets_of(n, h)

    plan = list(PLAN) if (levels, chunks) == (4, 4) else []
    for stage in range(levels + 2):
        for n in range(chunks):
            for h in range(2):
                if (stage, n, h) not in plan:
                    plan.append((stage, n, h))
    for stage, n, h in plan:
        run(stage, n, h)

    for level in range(levels):
        for n in range(chunks):
            for h in range(2):
                for copy in exchange(level, n, h):
                    copy.wait_send()
    each_share(lambda copy: copy.wait_send())
    for copy in finals:
        copy.wait()


def shards(rhs, leaf_basis, transfer, ranks, out_basis):
    leaves, rank_cap, width = leaf_basis.shape
    points = width // 2
    columns = rhs.shape[1]
    levels = transfer.shape[0]
    n_col = lax.axis_size("col")
    owned = leaves // n_col
    block_count = 1 << levels
    half = block_count // 2
    chunks = leaves // block_count
    piece = min(block_count, owned)
    sizes = (levels, chunks, owned, n_col, points, rank_cap)
    any_space = pl.BlockSpec(memory_space=pl.ANY)
    result = pl.pallas_call(
        functools.partial(kernel, sizes),
        out_shape=jax.ShapeDtypeStruct((owned, points, columns), BF16),
        in_specs=[pl.BlockSpec(memory_space=pltpu.SMEM)] + [any_space] * 4,
        out_specs=any_space,
        scratch_shapes=[
            pltpu.VMEM((chunks, block_count, points, columns), BF16),
            pltpu.VMEM((chunks, block_count, rank_cap, width), BF16),
            pltpu.VMEM((levels, leaves // 2, 2 * rank_cap, 4 * rank_cap), BF16),
            pltpu.VMEM((owned, points, 2 * rank_cap), BF16),
            pltpu.VMEM((owned, points, columns), BF16),
            pltpu.VMEM((levels + 1, chunks, block_count, rank_cap, columns), F32),
            pltpu.VMEM((levels, chunks, half, rank_cap, columns), F32),
            pltpu.VMEM((n_col, owned, rank_cap, columns), F32),
            pltpu.SemaphoreType.DMA((2 * chunks + levels + 1,)),
            pltpu.SemaphoreType.DMA((owned // piece, 2)),
            pltpu.SemaphoreType.DMA((levels, chunks, 2, 2)),
            pltpu.SemaphoreType.DMA((levels, chunks, 2, 2)),
            pltpu.SemaphoreType.DMA((chunks, block_count // piece)),
            pltpu.SemaphoreType.DMA((n_col, owned // piece)),
        ],
        compiler_params=pltpu.CompilerParams(
            collective_id=0, has_side_effects=True, vmem_limit_bytes=56 * 1024 * 1024
        ),
    )(
        ranks.reshape(levels, leaves),
        rhs.reshape(block_count, chunks, points, columns),
        leaf_basis.reshape(block_count, chunks, rank_cap, width),
        transfer.reshape(levels, leaves // 2, 2 * rank_cap, 4 * rank_cap),
        out_basis.reshape(leaves, points, 2 * rank_cap),
    )
    return result.reshape(owned * points, columns)


def solution(mesh):
    in_specs = (
        P(("row", "col"), None),
        P(("row", "col"), None, None),
        P(None, "row", "col", None, None, None),
        P(None, "row", "col", None),
        P("row", None, None, None),
    )
    out_specs = P(("row", "col"), None)
    return jax.shard_map(shards, mesh=mesh, in_specs=in_specs, out_specs=out_specs, check_vma=False)
```

```python
import functools

import jax
import jax.numpy as jnp
from jax import lax
from jax.experimental import pallas as pl
from jax.experimental.pallas import tpu as pltpu
from jax.sharding import PartitionSpec as P

MESH = pl.DeviceIdType.MESH
F32 = jnp.float32
BF16 = jnp.bfloat16
PLAN = (
    (0, 0, 0), (0, 0, 1), (0, 1, 0), (1, 0, 0), (1, 0, 1), (0, 1, 1),
    (1, 1, 0), (1, 1, 1), (2, 0, 0), (0, 2, 0), (0, 2, 1), (1, 2, 0),
    (2, 0, 1), (1, 2, 1), (3, 0, 0), (0, 3, 0), (2, 1, 0), (0, 3, 1),
    (1, 3, 0), (2, 1, 1), (1, 3, 1), (3, 1, 0), (2, 2, 0), (2, 2, 1),
    (3, 0, 1), (4, 0, 0), (3, 2, 0), (2, 3, 0), (2, 3, 1), (4, 0, 1),
    (3, 1, 1), (4, 1, 0), (3, 3, 0), (4, 1, 1), (3, 2, 1), (4, 2, 0),
    (4, 2, 1), (5, 2, 0), (5, 2, 1), (3, 3, 1), (4, 3, 0), (5, 3, 0),
    (4, 3, 1), (5, 3, 1),
)


def rotated(z):
    middle = z.shape[1] // 2
    lane = lax.broadcasted_iota(jnp.int32, z.shape, 1)
    turned = pltpu.roll(z, middle, 1)
    return jnp.where(lane < middle, -turned, turned)


def split_dot(matrix, stacked):
    high = stacked.astype(BF16)
    low = (stacked - high.astype(F32)).astype(BF16)
    both = jnp.dot(matrix, jnp.concatenate([high, low], 1), preferred_element_type=F32)
    columns = stacked.shape[1]
    return both[:, :columns] + both[:, columns:]


def kernel(
    sizes, ranks, rhs_hbm, leaf_hbm, transfer_hbm, basis_hbm, result_hbm,
    rhs, leaf, transfer, basis, result, coeff, arrived, shared,
    load_sem, out_sem, send_sem, recv_sem, share_send, share_recv,
):
    levels, chunks, owned, n_col, points, rank_cap = sizes
    block_count = 1 << levels
    half = block_count // 2
    quarter = half // 2
    p = lax.axis_index("row")
    c = lax.axis_index("col")
    bits = [(p // (1 << level)) % 2 for level in range(levels)] + [1]
    partners = [p + (1 - 2 * bits[level]) * (1 << level) for level in range(levels)]
    piece = min(block_count, owned)
    own_chunks = max(1, chunks // n_col)
    first = (c * chunks) // n_col + own_chunks
    order = [(first + n) % chunks for n in range(chunks)]

    loads = {}

    def load(name, source, target):
        copy = pltpu.make_async_copy(source, target, load_sem.at[len(loads)])
        copy.start()
        loads[name] = copy

    for n in range(chunks):
        load(("rhs", n), rhs_hbm.at[:, order[n]], rhs.at[n])
        load(("leaf", n), leaf_hbm.at[:, order[n]], leaf.at[n])
        if n == 0:
            load(("transfer", 0), transfer_hbm.at[0], transfer.at[0])
    for level in range(1, levels):
        load(("transfer", level), transfer_hbm.at[level], transfer.at[level])
    load("basis", basis_hbm.at[pl.ds(c * owned, owned)], basis)

    barrier = pltpu.get_barrier_semaphore()
    for level in range(levels):
        pl.semaphore_signal(barrier, 1, device_id={"row": partners[level]}, device_id_type=MESH)
    for step in range(1, n_col):
        pl.semaphore_signal(barrier, 1, device_id={"col": (c + step) % n_col}, device_id_type=MESH)
    pl.semaphore_wait(barrier, levels + n_col - 1)

    waited = set()

    def loaded(name):
        if name not in waited:
            waited.add(name)
            loads[name].wait()

    def part(level, h):
        if level == levels - 1:
            return h
        return 1 - bits[level + 1] if h == 0 else bits[level + 1]

    def exchange(level, n, h):
        count = 2 if n == 0 and 0 < level < levels - 1 else 1
        size = quarter // count
        copies = []
        for k in range(count):
            at = part(level, h) * quarter + (part(level + 1, k) * size if count == 2 else 0)
            copies.append(
                pltpu.make_async_remote_copy(
                    src_ref=coeff.at[level, n, pl.ds((1 - bits[level]) * half + at, size)],
                    dst_ref=arrived.at[level, n, pl.ds(at, size)],
                    send_sem=send_sem.at[level, n, h, k],
                    recv_sem=recv_sem.at[level, n, h, k],
                    device_id={"row": partners[level]},
                    device_id_type=MESH,
                )
            )
        return copies

    def send(level, n, h):
        for copy in exchange(level, n, h):
            copy.start()

    def in_loop(count, act):
        width = min(4, count)

        def body(i, carry):
            stores = [act(width * i + u) for u in range(width)]
            for ref, rows in stores:
                for at, block in rows:
                    ref[at] = block
            return carry

        if count == width:
            body(0, 0)
        else:
            lax.fori_loop(0, count // width, body, 0)

    def leaf_block(n, f):
        matrix = leaf[n, f]
        parts = jnp.concatenate([matrix[:, :points], matrix[:, points:]], 0)
        both = jnp.dot(parts, rhs[n, f], preferred_element_type=F32)
        return coeff, [((0, n, f), both[:rank_cap] + rotated(both[rank_cap:]))]

    def leaf_blocks(n, start, count):
        in_loop(count, lambda i: leaf_block(n, start + i))

    def mix_block(level, n, m):
        low = m % (1 << level)
        high = m // (1 << level)
        j = high * (chunks << level) + order[n] * (1 << level) + low
        own = coeff[level, n, bits[level] * half + m]
        other = arrived[level, n, m]
        stacked = jnp.concatenate([own, rotated(own), other, rotated(other)], 0)
        mixed = split_dot(transfer[level, j], stacked)
        row = lax.broadcasted_iota(jnp.int32, (rank_cap, mixed.shape[1]), 0)
        rows = []
        for s in range(2):
            live = row < ranks[level, 2 * j + s]
            block = jnp.where(live, mixed[s * rank_cap : (s + 1) * rank_cap], 0.0)
            rows.append(((level + 1, n, 2 * m + s), block))
        return coeff, rows

    def mix_blocks(level, n, start, count):
        in_loop(count, lambda i: mix_block(level, n, start + i))

    def leaves_of(n, h):
        loaded(("rhs", n))
        loaded(("leaf", n))
        if h == 1:
            leaf_blocks(n, bits[0] * half, half)
            return
        sent = (1 - bits[0]) * half
        for k in range(2):
            leaf_blocks(n, sent + part(0, k) * quarter, quarter)
            send(0, n, k)

    def mix(level, n, h):
        loaded(("transfer", level))
        copies = exchange(level, n, h)
        start = part(level, h) * quarter
        if h == 1 or level + 1 == levels:
            for copy in copies:
                copy.wait_recv()
            mix_blocks(level, n, start, quarter)
            return
        for k in range(2):
            if k < len(copies):
                copies[k].wait_recv()
            mix_blocks(level, n, start + part(level + 1, k) * (quarter // 2), quarter // 2)
            if k == 0 or level + 1 != levels - 2:
                send(level + 1, n, k)
        if level == levels - 2:
            send(level, n, 1)

    def share(n, k):
        g = order[n] * block_count + k * piece
        owner = g // owned
        slot = (g % owned) // piece
        return owner, pltpu.make_async_remote_copy(
            src_ref=coeff.at[levels, n, pl.ds(k * piece, piece)],
            dst_ref=shared.at[c, pl.ds(slot * piece, piece)],
            send_sem=share_send.at[n, k],
            recv_sem=share_recv.at[c, slot],
            device_id={"col": owner},
            device_id_type=MESH,
        )

    pieces = block_count // piece

    def each_share(act):
        for n in range(chunks):
            act_on_share(n, act)

    def act_on_share(n, act):
        if chunks >= n_col:
            if n < chunks - own_chunks:
                act(share(n, 0)[1])
            return
        for k in range(pieces):
            owner, copy = share(n, k)

            @pl.when(owner != c)
            def _():
                act(copy)

    def share_out(n):
        act_on_share(n, lambda copy: copy.start())

    def receive_shares(slot):
        for step in range(1, n_col):
            sender = (c + step) % n_col
            pltpu.make_async_remote_copy(
                src_ref=coeff.at[levels, 0, pl.ds(0, piece)],
                dst_ref=shared.at[sender, pl.ds(slot * piece, piece)],
                send_sem=share_send.at[0, 0],
                recv_sem=share_recv.at[sender, slot],
                device_id={"col": sender},
                device_id_type=MESH,
            ).wait_recv()

    def target_block(n, f, g):
        total = coeff[levels, n, f]
        for step in range(1, n_col):
            total = total + shared[(c + step) % n_col, g]
        stacked = jnp.concatenate([total, rotated(total)], 0)
        return result, [(g, split_dot(basis[g], stacked).astype(BF16))]

    def targets_of(n, h):
        slot = n - (chunks - own_chunks)
        begin, count = h * half, half
        if piece < block_count:
            if h == 0:
                return
            begin, count = (c * owned) % block_count, piece
        if h == 0 or piece < block_count:
            loaded("basis")
            receive_shares(slot)
        g = slot * piece + (h * half if piece == block_count else 0)
        in_loop(count, lambda i: target_block(n, begin + i, g + i))
        copy = pltpu.make_async_copy(
            result.at[pl.ds(g, count)], result_hbm.at[pl.ds(g, count)], out_sem.at[slot, h]
        )
        copy.start()
        finals.append(copy)

    finals = []

    def run(stage, n, h):
        if stage == 0:
            leaves_of(n, h)
        elif stage <= levels:
            mix(stage - 1, n, h)
            if stage == levels and h == 1:
                share_out(n)
        elif n >= chunks - own_chunks:
            targets_of(n, h)

    plan = list(PLAN) if (levels, chunks) == (4, 4) else []
    for stage in range(levels + 2):
        for n in range(chunks):
            for h in range(2):
                if (stage, n, h) not in plan:
                    plan.append((stage, n, h))
    for stage, n, h in plan:
        run(stage, n, h)

    for level in range(levels):
        for n in range(chunks):
            for h in range(2):
                for copy in exchange(level, n, h):
                    copy.wait_send()
    each_share(lambda copy: copy.wait_send())
    for copy in finals:
        copy.wait()


def shards(rhs, leaf_basis, transfer, ranks, out_basis):
    leaves, rank_cap, width = leaf_basis.shape
    points = width // 2
    columns = rhs.shape[1]
    levels = transfer.shape[0]
    n_col = lax.axis_size("col")
    owned = leaves // n_col
    block_count = 1 << levels
    half = block_count // 2
    chunks = leaves // block_count
    piece = min(block_count, owned)
    sizes = (levels, chunks, owned, n_col, points, rank_cap)
    any_space = pl.BlockSpec(memory_space=pl.ANY)
    result = pl.pallas_call(
        functools.partial(kernel, sizes),
        out_shape=jax.ShapeDtypeStruct((owned, points, columns), BF16),
        in_specs=[pl.BlockSpec(memory_space=pltpu.SMEM)] + [any_space] * 4,
        out_specs=any_space,
        scratch_shapes=[
            pltpu.VMEM((chunks, block_count, points, columns), BF16),
            pltpu.VMEM((chunks, block_count, rank_cap, width), BF16),
            pltpu.VMEM((levels, leaves // 2, 2 * rank_cap, 4 * rank_cap), BF16),
            pltpu.VMEM((owned, points, 2 * rank_cap), BF16),
            pltpu.VMEM((owned, points, columns), BF16),
            pltpu.VMEM((levels + 1, chunks, block_count, rank_cap, columns), F32),
            pltpu.VMEM((levels, chunks, half, rank_cap, columns), F32),
            pltpu.VMEM((n_col, owned, rank_cap, columns), F32),
            pltpu.SemaphoreType.DMA((2 * chunks + levels + 1,)),
            pltpu.SemaphoreType.DMA((owned // piece, 2)),
            pltpu.SemaphoreType.DMA((levels, chunks, 2, 2)),
            pltpu.SemaphoreType.DMA((levels, chunks, 2, 2)),
            pltpu.SemaphoreType.DMA((chunks, block_count // piece)),
            pltpu.SemaphoreType.DMA((n_col, owned // piece)),
        ],
        compiler_params=pltpu.CompilerParams(
            collective_id=0, has_side_effects=True, vmem_limit_bytes=56 * 1024 * 1024
        ),
    )(
        ranks.reshape(levels, leaves),
        rhs.reshape(block_count, chunks, points, columns),
        leaf_basis.reshape(block_count, chunks, rank_cap, width),
        transfer.reshape(levels, leaves // 2, 2 * rank_cap, 4 * rank_cap),
        out_basis.reshape(leaves, points, 2 * rank_cap),
    )
    return result.reshape(owned * points, columns)


def solution(mesh):
    in_specs = (
        P(("row", "col"), None),
        P(("row", "col"), None, None),
        P(None, "row", "col", None, None, None),
        P(None, "row", "col", None),
        P("row", None, None, None),
    )
    out_specs = P(("row", "col"), None)
    return jax.shard_map(shards, mesh=mesh, in_specs=in_specs, out_specs=out_specs, check_vma=False)
```

```python
import functools

import jax
import jax.numpy as jnp
from jax import lax
from jax.experimental import pallas as pl
from jax.experimental.pallas import tpu as pltpu
from jax.sharding import PartitionSpec as P

MESH = pl.DeviceIdType.MESH
F32 = jnp.float32
BF16 = jnp.bfloat16
PLAN = (
    (0, 0, 0), (0, 0, 1), (0, 1, 0), (1, 0, 0), (1, 0, 1), (0, 1, 1),
    (1, 1, 0), (1, 1, 1), (2, 0, 0), (0, 2, 0), (0, 2, 1), (1, 2, 0),
    (2, 0, 1), (1, 2, 1), (3, 0, 0), (0, 3, 0), (2, 1, 0), (0, 3, 1),
    (1, 3, 0), (2, 1, 1), (1, 3, 1), (3, 1, 0), (2, 2, 0), (2, 2, 1),
    (3, 0, 1), (3, 2, 0), (2, 3, 0), (2, 3, 1), (4, 0, 0), (4, 0, 1),
    (3, 3, 0), (3, 1, 1), (4, 1, 0), (4, 1, 1), (3, 2, 1), (4, 2, 0),
    (4, 2, 1), (5, 2, 0), (5, 2, 1), (3, 3, 1), (4, 3, 0), (5, 3, 0),
    (4, 3, 1), (5, 3, 1),
)


def rotated(z):
    middle = z.shape[1] // 2
    lane = lax.broadcasted_iota(jnp.int32, z.shape, 1)
    turned = pltpu.roll(z, middle, 1)
    return jnp.where(lane < middle, -turned, turned)


def split_dot(matrix, stacked):
    high = stacked.astype(BF16)
    low = (stacked - high.astype(F32)).astype(BF16)
    both = jnp.dot(matrix, jnp.concatenate([high, low], 1), preferred_element_type=F32)
    columns = stacked.shape[1]
    return both[:, :columns] + both[:, columns:]


def kernel(
    sizes, ranks, rhs_hbm, leaf_hbm, transfer_hbm, basis_hbm, result_hbm,
    rhs, leaf, transfer, basis, result, coeff, arrived, shared,
    load_sem, out_sem, send_sem, recv_sem, share_send, share_recv,
):
    levels, chunks, owned, n_col, points, rank_cap = sizes
    block_count = 1 << levels
    half = block_count // 2
    quarter = half // 2
    p = lax.axis_index("row")
    c = lax.axis_index("col")
    bits = [(p // (1 << level)) % 2 for level in range(levels)] + [1]
    partners = [p + (1 - 2 * bits[level]) * (1 << level) for level in range(levels)]
    piece = min(block_count, owned)
    own_chunks = max(1, chunks // n_col)
    first = (c * chunks) // n_col + own_chunks
    order = [(first + n) % chunks for n in range(chunks)]

    loads = {}

    def load(name, source, target):
        copy = pltpu.make_async_copy(source, target, load_sem.at[len(loads)])
        copy.start()
        loads[name] = copy

    for n in range(chunks):
        load(("rhs", n), rhs_hbm.at[:, order[n]], rhs.at[n])
        load(("leaf", n), leaf_hbm.at[:, order[n]], leaf.at[n])
        if n == 0:
            load(("transfer", 0), transfer_hbm.at[0], transfer.at[0])
    for level in range(1, levels):
        load(("transfer", level), transfer_hbm.at[level], transfer.at[level])
    load("basis", basis_hbm.at[pl.ds(c * owned, owned)], basis)

    barrier = pltpu.get_barrier_semaphore()
    for level in range(levels):
        pl.semaphore_signal(barrier, 1, device_id={"row": partners[level]}, device_id_type=MESH)
    for step in range(1, n_col):
        pl.semaphore_signal(barrier, 1, device_id={"col": (c + step) % n_col}, device_id_type=MESH)
    pl.semaphore_wait(barrier, levels + n_col - 1)

    waited = set()

    def loaded(name):
        if name not in waited:
            waited.add(name)
            loads[name].wait()

    def part(level, h):
        if level == levels - 1:
            return h
        return 1 - bits[level + 1] if h == 0 else bits[level + 1]

    def exchange(level, n, h):
        count = 2 if n == 0 and 0 < level < levels - 1 else 1
        size = quarter // count
        copies = []
        for k in range(count):
            at = part(level, h) * quarter + (part(level + 1, k) * size if count == 2 else 0)
            copies.append(
                pltpu.make_async_remote_copy(
                    src_ref=coeff.at[level, n, pl.ds((1 - bits[level]) * half + at, size)],
                    dst_ref=arrived.at[level, n, pl.ds(at, size)],
                    send_sem=send_sem.at[level, n, h, k],
                    recv_sem=recv_sem.at[level, n, h, k],
                    device_id={"row": partners[level]},
                    device_id_type=MESH,
                )
            )
        return copies

    def send(level, n, h):
        for copy in exchange(level, n, h):
            copy.start()

    def in_loop(count, act):
        width = min(4, count)

        def body(i, carry):
            stores = [act(width * i + u) for u in range(width)]
            for ref, rows in stores:
                for at, block in rows:
                    ref[at] = block
            return carry

        if count == width:
            body(0, 0)
        else:
            lax.fori_loop(0, count // width, body, 0)

    def leaf_block(n, f):
        matrix = leaf[n, f]
        parts = jnp.concatenate([matrix[:, :points], matrix[:, points:]], 0)
        both = jnp.dot(parts, rhs[n, f], preferred_element_type=F32)
        return coeff, [((0, n, f), both[:rank_cap] + rotated(both[rank_cap:]))]

    def leaf_blocks(n, start, count):
        in_loop(count, lambda i: leaf_block(n, start + i))

    def mix_block(level, n, m):
        low = m % (1 << level)
        high = m // (1 << level)
        j = high * (chunks << level) + order[n] * (1 << level) + low
        own = coeff[level, n, bits[level] * half + m]
        other = arrived[level, n, m]
        stacked = jnp.concatenate([own, rotated(own), other, rotated(other)], 0)
        mixed = split_dot(transfer[level, j], stacked)
        row = lax.broadcasted_iota(jnp.int32, (rank_cap, mixed.shape[1]), 0)
        rows = []
        for s in range(2):
            live = row < ranks[level, 2 * j + s]
            block = jnp.where(live, mixed[s * rank_cap : (s + 1) * rank_cap], 0.0)
            rows.append(((level + 1, n, 2 * m + s), block))
        return coeff, rows

    def mix_blocks(level, n, start, count):
        in_loop(count, lambda i: mix_block(level, n, start + i))

    def leaves_of(n, h):
        loaded(("rhs", n))
        loaded(("leaf", n))
        if h == 1:
            leaf_blocks(n, bits[0] * half, half)
            return
        sent = (1 - bits[0]) * half
        for k in range(2):
            leaf_blocks(n, sent + part(0, k) * quarter, quarter)
            send(0, n, k)

    def mix(level, n, h):
        loaded(("transfer", level))
        copies = exchange(level, n, h)
        start = part(level, h) * quarter
        if h == 1 or level + 1 == levels:
            for copy in copies:
                copy.wait_recv()
            mix_blocks(level, n, start, quarter)
            return
        for k in range(2):
            if k < len(copies):
                copies[k].wait_recv()
            mix_blocks(level, n, start + part(level + 1, k) * (quarter // 2), quarter // 2)
            if k == 0 or level + 1 != levels - 2:
                send(level + 1, n, k)
        if level == levels - 2:
            send(level, n, 1)

    def share(n, k):
        g = order[n] * block_count + k * piece
        owner = g // owned
        slot = (g % owned) // piece
        return owner, pltpu.make_async_remote_copy(
            src_ref=coeff.at[levels, n, pl.ds(k * piece, piece)],
            dst_ref=shared.at[c, pl.ds(slot * piece, piece)],
            send_sem=share_send.at[n, k],
            recv_sem=share_recv.at[c, slot],
            device_id={"col": owner},
            device_id_type=MESH,
        )

    pieces = block_count // piece

    def each_share(act):
        for n in range(chunks):
            act_on_share(n, act)

    def act_on_share(n, act):
        if chunks >= n_col:
            if n < chunks - own_chunks:
                act(share(n, 0)[1])
            return
        for k in range(pieces):
            owner, copy = share(n, k)

            @pl.when(owner != c)
            def _():
                act(copy)

    def share_out(n):
        act_on_share(n, lambda copy: copy.start())

    def receive_shares(slot):
        for step in range(1, n_col):
            sender = (c + step) % n_col
            pltpu.make_async_remote_copy(
                src_ref=coeff.at[levels, 0, pl.ds(0, piece)],
                dst_ref=shared.at[sender, pl.ds(slot * piece, piece)],
                send_sem=share_send.at[0, 0],
                recv_sem=share_recv.at[sender, slot],
                device_id={"col": sender},
                device_id_type=MESH,
            ).wait_recv()

    def target_block(n, f, g):
        total = coeff[levels, n, f]
        for step in range(1, n_col):
            total = total + shared[(c + step) % n_col, g]
        stacked = jnp.concatenate([total, rotated(total)], 0)
        return result, [(g, split_dot(basis[g], stacked).astype(BF16))]

    def targets_of(n, h):
        slot = n - (chunks - own_chunks)
        begin, count = h * half, half
        if piece < block_count:
            if h == 0:
                return
            begin, count = (c * owned) % block_count, piece
        if h == 0 or piece < block_count:
            loaded("basis")
            receive_shares(slot)
        g = slot * piece + (h * half if piece == block_count else 0)
        in_loop(count, lambda i: target_block(n, begin + i, g + i))
        copy = pltpu.make_async_copy(
            result.at[pl.ds(g, count)], result_hbm.at[pl.ds(g, count)], out_sem.at[slot, h]
        )
        copy.start()
        finals.append(copy)

    finals = []

    def run(stage, n, h):
        if stage == 0:
            leaves_of(n, h)
        elif stage <= levels:
            mix(stage - 1, n, h)
            if stage == levels and h == 1:
                share_out(n)
        elif n >= chunks - own_chunks:
            targets_of(n, h)

    plan = list(PLAN) if (levels, chunks) == (4, 4) else []
    for stage in range(levels + 2):
        for n in range(chunks):
            for h in range(2):
                if (stage, n, h) not in plan:
                    plan.append((stage, n, h))
    for stage, n, h in plan:
        run(stage, n, h)

    for level in range(levels):
        for n in range(chunks):
            for h in range(2):
                for copy in exchange(level, n, h):
                    copy.wait_send()
    each_share(lambda copy: copy.wait_send())
    for copy in finals:
        copy.wait()


def shards(rhs, leaf_basis, transfer, ranks, out_basis):
    leaves, rank_cap, width = leaf_basis.shape
    points = width // 2
    columns = rhs.shape[1]
    levels = transfer.shape[0]
    n_col = lax.axis_size("col")
    owned = leaves // n_col
    block_count = 1 << levels
    half = block_count // 2
    chunks = leaves // block_count
    piece = min(block_count, owned)
    sizes = (levels, chunks, owned, n_col, points, rank_cap)
    any_space = pl.BlockSpec(memory_space=pl.ANY)
    result = pl.pallas_call(
        functools.partial(kernel, sizes),
        out_shape=jax.ShapeDtypeStruct((owned, points, columns), BF16),
        in_specs=[pl.BlockSpec(memory_space=pltpu.SMEM)] + [any_space] * 4,
        out_specs=any_space,
        scratch_shapes=[
            pltpu.VMEM((chunks, block_count, points, columns), BF16),
            pltpu.VMEM((chunks, block_count, rank_cap, width), BF16),
            pltpu.VMEM((levels, leaves // 2, 2 * rank_cap, 4 * rank_cap), BF16),
            pltpu.VMEM((owned, points, 2 * rank_cap), BF16),
            pltpu.VMEM((owned, points, columns), BF16),
            pltpu.VMEM((levels + 1, chunks, block_count, rank_cap, columns), F32),
            pltpu.VMEM((levels, chunks, half, rank_cap, columns), F32),
            pltpu.VMEM((n_col, owned, rank_cap, columns), F32),
            pltpu.SemaphoreType.DMA((2 * chunks + levels + 1,)),
            pltpu.SemaphoreType.DMA((owned // piece, 2)),
            pltpu.SemaphoreType.DMA((levels, chunks, 2, 2)),
            pltpu.SemaphoreType.DMA((levels, chunks, 2, 2)),
            pltpu.SemaphoreType.DMA((chunks, block_count // piece)),
            pltpu.SemaphoreType.DMA((n_col, owned // piece)),
        ],
        compiler_params=pltpu.CompilerParams(
            collective_id=0, has_side_effects=True, vmem_limit_bytes=56 * 1024 * 1024
        ),
    )(
        ranks.reshape(levels, leaves),
        rhs.reshape(block_count, chunks, points, columns),
        leaf_basis.reshape(block_count, chunks, rank_cap, width),
        transfer.reshape(levels, leaves // 2, 2 * rank_cap, 4 * rank_cap),
        out_basis.reshape(leaves, points, 2 * rank_cap),
    )
    return result.reshape(owned * points, columns)


def solution(mesh):
    in_specs = (
        P(("row", "col"), None),
        P(("row", "col"), None, None),
        P(None, "row", "col", None, None, None),
        P(None, "row", "col", None),
        P("row", None, None, None),
    )
    out_specs = P(("row", "col"), None)
    return jax.shard_map(shards, mesh=mesh, in_specs=in_specs, out_specs=out_specs, check_vma=False)
```
